32 devices in a mesh: dev: 32 (over z, y, x, core).
Axes of the slice: x: 2, y: 2, z: 4, core: 2. Of those that a mesh axis runs over, the one named last changes fastest.
Arguments:
- tokens: bfloat16 [24576, 1024], P('dev'), may hold values from -6 to 6
- seq_ids: int32 [24576], P('dev'), may hold values from 0 to 32, as said below
- positions: int32 [24576], P('dev'), may hold values from 0 to 1406, as said below
- w_qkv: bfloat16 [1024, 3072], P('dev'), may hold values from -0.1875 to 0.1875
- w_out: bfloat16 [1024, 1024], P('dev'), may hold values from -1.5 to 1.5
- w_in: bfloat16 [1024, 5248], P('dev'), may hold values from -0.1875 to 0.1875
- w_down: bfloat16 [2624, 1024], P(None, 'dev'), may hold values from -0.15625 to 0.15625
- gain_attn: bfloat16 [1024], P('dev'), may hold values from 0.099609375 to 1.8984375
- gain_mlp: bfloat16 [1024], P('dev'), may hold values from 0.099609375 to 1.8984375
- cotangent: bfloat16 [24576, 1024], P('dev'), may hold values from -6 to 6
Outputs:
- layer_out: bfloat16 [24576, 1024], P('dev')
- tokens_grad: bfloat16 [24576, 1024], P('dev')
- qkv_grad: float32 [1024, 3072], P('dev')
- out_grad: float32 [1024, 1024], P('dev')
- in_grad: float32 [1024, 5248], P('dev')
- down_grad: float32 [2624, 1024], P(None, 'dev')
- attn_gain_grad: float32 [1024], P('dev')
- mlp_gain_grad: float32 [1024], P('dev')
The draws below stay inside these ranges and needn't reach their ends.
Inputs may be any that keep to these rules, and one draw needn't show every extreme that they name: `seq_ids`: sequence numbers rise along the tokens from 0; every device's rows hold exactly one sequence start, at least 64 rows from either end of its rows, so the first and last 64 rows of a device lie in one sequence together with the 64 rows beyond them on the neighbouring device. `positions`: position within the sequence: 0 at a sequence's first token, rising by one.
All inputs are finite; a program needn't handle non-finite values.
Results may differ from the reference program's by a relative error of at most 0.017.
Values may be sent and summed in bfloat16 or wider, within the bound.
A program may use at most 256 MiB of HBM per device.

```python
import math
import jax
import jax.numpy as jnp
from jax import lax

D = 1024
HDIM = 64
FF = 2624
HALF = 64
TOK_DEV = 768
TOKENS = 24576
N_DEV = 32


def boundary_places(key):
    place_key, pick_key = jax.random.split(key)
    places = jax.random.randint(place_key, (N_DEV,), HALF, TOK_DEV - HALF).astype(jnp.int32)
    chosen = jax.random.randint(pick_key, (), 0, N_DEV - 1).astype(jnp.int32)
    device = jnp.arange(N_DEV, dtype=jnp.int32)
    places = jnp.where(device == chosen, HALF, places)
    places = jnp.where(device == chosen + 1, TOK_DEV - HALF - 1, places)
    return places.astype(jnp.int32)


def draw_seq_ids(key, part):
    places = boundary_places(key)
    local = jnp.arange(TOK_DEV, dtype=jnp.int32)[None, :]
    device = jnp.arange(N_DEV, dtype=jnp.int32)[:, None]
    numbers = device + (local >= places[:, None]).astype(jnp.int32)
    return numbers.reshape(-1).astype(jnp.int32)


def draw_positions(key, part):
    places = boundary_places(key)
    local = jnp.arange(TOK_DEV, dtype=jnp.int32)[None, :]
    previous = jnp.concatenate([jnp.full((1,), TOK_DEV, jnp.int32), places[:-1]])
    within = jnp.where(local >= places[:, None], local - places[:, None], local + TOK_DEV - previous[:, None])
    return within.reshape(-1).astype(jnp.int32)


def strengthened(entries, stream_key, source, target, shards_of, factor):
    owner, partner = [(jnp.arange(entries.shape[dim]) // (entries.shape[dim] // shards_of)).reshape([-1 if axis == dim else 1 for axis in range(entries.ndim)]) for dim in (source, target)]
    chosen = jax.random.permutation(stream_key, shards_of)[partner]
    strong = (owner == chosen) | (owner == (partner + shards_of // 2) % shards_of)
    return jnp.where(strong, factor * entries, entries)


def block_scale(key, dims, cuts, smallest, high):
    level = 1.0
    for position, blocks in cuts:
        steps = jax.random.uniform(jax.random.fold_in(jax.random.fold_in(key, 6), position), (blocks,), jnp.float32, smallest / len(cuts), high / len(cuts))
        level = level * jnp.repeat(jnp.exp(steps), dims[position] // blocks).reshape((-1,) + (1,) * (len(dims) - 1 - position))
    return level


def noise(stream_key, dims, deviation, reach, pieces=(), held_as=jnp.bfloat16):
    array = deviation * jax.random.normal(stream_key, dims, jnp.float32)
    if pieces:
        array = array * block_scale(stream_key, dims, pieces, -0.22, 0.18)
    return jnp.clip(array, -reach, reach).astype(held_as)


def heavy_noise(own_key, shape, width, reach, cuts, heavy, kind=jnp.bfloat16):
    array = width * jax.random.normal(own_key, shape, jnp.float32)
    if cuts:
        array = array * block_scale(own_key, shape, cuts, -0.22, 0.18)
    return jnp.clip(strengthened(array, jax.random.fold_in(own_key, 3), *heavy), -reach, reach).astype(kind)


def setup_inputs(seed: int = 0) -> dict:
    streams_of = jax.random.split(jax.random.key(seed), 11)
    tokens = noise(streams_of[0], (TOKENS, D), 1.0, 6.0, ((0, 32),))
    seq_ids = draw_seq_ids(jax.random.fold_in(streams_of[10], 71), 0)
    positions = draw_positions(jax.random.fold_in(streams_of[10], 71), 0)
    w_qkv = noise(streams_of[3], (D, 3 * D), D ** -0.5, 0.1875, ((0, 32),))
    w_out = noise(streams_of[4], (D, D), (D // 64) ** -0.5, 1.5, ((0, 32),))
    w_in = noise(streams_of[5], (D, 2 * FF), D ** -0.5, 0.1875, ((0, 32),))
    w_down = noise(streams_of[6], (FF, D), (FF // 2) ** -0.5, 0.15625, ((1, 32),))
    gain_attn = jnp.clip(1.0 + 0.18 * jax.random.normal(streams_of[7], (D,), jnp.float32), 0.099609375, 1.8984375).astype(jnp.bfloat16)
    gain_mlp = jnp.clip(1.0 + 0.18 * jax.random.normal(streams_of[8], (D,), jnp.float32), 0.099609375, 1.8984375).astype(jnp.bfloat16)
    cotangent = heavy_noise(streams_of[9], (TOKENS, D), 1.0, 6.0, ((0, 32),), (0, 1, 32, 2.75))
    return {"tokens": tokens, "seq_ids": seq_ids, "positions": positions, "w_qkv": w_qkv, "w_out": w_out, "w_in": w_in, "w_down": w_down, "gain_attn": gain_attn, "gain_mlp": gain_mlp, "cotangent": cotangent}


epsilon = 1e-05
masked_score = -1e+30

@jax.custom_vjp
def low(v):
    return lax.optimization_barrier(v.astype(jnp.bfloat16)).astype(jnp.float32)

@jax.custom_vjp
def low_back(v):
    return v

def low_keep(v):
    return (low(v), None)

def low_pass(kept, grad):
    return (grad,)

def back_keep(v):
    return (v, None)

def back_low(kept, grad):
    return (low(grad),)
low.defvjp(low_keep, low_pass)
low_back.defvjp(back_keep, back_low)

def layer_norm(values):
    centred = values - lax.optimization_barrier(jnp.mean(values, axis=-1, keepdims=True))
    return centred * lax.rsqrt(lax.optimization_barrier(jnp.mean(centred * centred, axis=-1, keepdims=True)) + epsilon)

def rope_tables(positions, head_size):
    half_size = head_size // 2
    inverse_freq = 10000.0 ** (-(jnp.arange(half_size).astype(jnp.float32) * 2.0 / head_size))
    angles = positions.astype(jnp.float32)[:, None] * inverse_freq[None, :]
    angles = jnp.concatenate([angles, angles], axis=-1)
    return (jnp.cos(angles)[:, None, :], jnp.sin(angles)[:, None, :])

def rotate_half(values):
    half_size = values.shape[-1] // 2
    return jnp.concatenate([-values[..., half_size:], values[..., :half_size]], axis=-1)

def apply_rope(values, cosine, sine_table):
    return values * cosine + rotate_half(values) * sine_table

def exact_dot(first_mat, second_mat):
    return jnp.dot(first_mat, second_mat, precision=lax.Precision.HIGHEST, preferred_element_type=jnp.float32)

def reference(tokens, seq_ids, positions, w_qkv, w_out, w_in, w_down, gain_attn, gain_mlp, cotangent):
    total_rows, model_width = tokens.shape
    head_count = model_width // HDIM
    query_block = math.gcd(TOK_DEV, 512)
    window_rows = query_block + 2 * HALF
    score_scale = 1.0 / math.sqrt(HDIM)
    cosine, sine_table = rope_tables(positions, HDIM)
    seq_ids = seq_ids.astype(jnp.int32)
    padded_ids = jnp.concatenate([jnp.full((HALF,), -1, jnp.int32), seq_ids, jnp.full((HALF,), -1, jnp.int32)])
    offsets = jnp.arange(query_block)[:, None] - jnp.arange(window_rows)[None, :] + HALF
    nearby = jnp.abs(offsets) <= HALF
    starts = jnp.arange(total_rows // query_block, dtype=jnp.int32) * query_block

    def forward(inputs, qkv_mat, out_mat, in_mat, down_mat, attn_gain, mlp_gain):
        h_attn = low(layer_norm(inputs) * attn_gain)
        projected = low_back(exact_dot(h_attn, qkv_mat))
        heads_split = projected.reshape(total_rows, 3, head_count, HDIM)
        queries = low(apply_rope(heads_split[:, 0], cosine, sine_table)).reshape(total_rows, model_width)
        keys_all = low(apply_rope(heads_split[:, 1], cosine, sine_table)).reshape(total_rows, model_width)
        values_all = low(heads_split[:, 2]).reshape(total_rows, model_width)
        keys_pad = jnp.pad(keys_all, ((HALF, HALF), (0, 0)))
        values_pad = jnp.pad(values_all, ((HALF, HALF), (0, 0)))

        def attend(block_start):
            query_tile = lax.dynamic_slice_in_dim(queries, block_start, query_block, 0).reshape(query_block, head_count, HDIM)
            key_tile = lax.dynamic_slice_in_dim(keys_pad, block_start, window_rows, 0).reshape(window_rows, head_count, HDIM)
            value_tile = lax.dynamic_slice_in_dim(values_pad, block_start, window_rows, 0).reshape(window_rows, head_count, HDIM)
            query_ids = lax.dynamic_slice_in_dim(seq_ids, block_start, query_block, 0)
            key_ids = lax.dynamic_slice_in_dim(padded_ids, block_start, window_rows, 0)
            allowed = nearby & (query_ids[:, None] == key_ids[None, :])
            scores = low_back(jnp.einsum('qhd,khd->hqk', query_tile, key_tile, precision=lax.Precision.HIGHEST) * score_scale)
            scores = jnp.where(allowed[None], scores, masked_score)
            row_peak = lax.optimization_barrier(jnp.max(scores, axis=-1, keepdims=True))
            exponent = jnp.exp(scores - row_peak)
            attn_probs = low(exponent / lax.optimization_barrier(jnp.sum(exponent, axis=-1, keepdims=True)))
            return jnp.einsum('hqk,khd->qhd', attn_probs, value_tile, precision=lax.Precision.HIGHEST).reshape(query_block, model_width)
        attended = lax.map(jax.checkpoint(attend), starts).reshape(total_rows, model_width)
        mixed = low_back(low(attended))
        residual = inputs + low_back(exact_dot(mixed, out_mat))
        h_mlp = low(layer_norm(residual) * mlp_gain)
        gate_up = low_back(exact_dot(h_mlp, in_mat))
        activated = low_back(low(jax.nn.gelu(gate_up[:, :FF], approximate=False) * gate_up[:, FF:]))
        return residual + exact_dot(activated, down_mat)
    result, backward = jax.vjp(forward, tokens.astype(jnp.float32), w_qkv.astype(jnp.float32), w_out.astype(jnp.float32), w_in.astype(jnp.float32), w_down.astype(jnp.float32), gain_attn.astype(jnp.float32), gain_mlp.astype(jnp.float32))
    gradients = backward(cotangent.astype(jnp.float32))
    return (result.astype(jnp.bfloat16), gradients[0].astype(jnp.bfloat16), gradients[1], gradients[2], gradients[3], gradients[4], gradients[5], gradients[6])
```

```python
import math

import jax
import jax.numpy as jnp
from jax import lax
from jax.sharding import PartitionSpec as P

HDIM = 64
HALF = 64


epsilon = 1e-05
masked_score = -1e30


def padded(cells, sides, width):
    for axis, dim in sides:
        count = lax.axis_size(axis)
        ends = count - 1
        head = lax.slice_in_dim(cells, 0, width, axis=dim)
        tail = lax.slice_in_dim(cells, cells.shape[dim] - width, cells.shape[dim], axis=dim)
        cells = jnp.concatenate(
            [
                lax.ppermute(tail, axis, [(i, (i + 1) % count) for i in range(ends)]),
                cells,
                lax.ppermute(head, axis, [((i + 1) % count, i) for i in range(ends)]),
            ],
            axis=dim,
        )
    return cells


def passed_along(value, axis, steps):
    count = lax.axis_size(axis)
    leading, last = (max(0, -steps), min(count, count - steps))
    return lax.ppermute(value, axis, [(source, source + steps) for source in range(leading, last)])


def swapped(value, count, mask):
    return lax.ppermute(value, "dev", [(i, i ^ mask) for i in range(count)])


def column_halves(width):
    middle = max(128, (width // 256) * 128)
    return ((0, middle, (2, 4)), (middle, width, (4, 2)))


def place_bits(dev_index):
    return {1: dev_index % 2, 2: (dev_index // 2) % 2, 4: (dev_index // 4) % 2}


def far_groups(count):
    return [list(range(first, count, 8)) for first in range(8)]


def gather_rows(shard):
    count = lax.axis_size("dev")
    dev_index = lax.axis_index("dev")
    bits = place_bits(dev_index)
    far = count // 8
    mine_far = dev_index // 8
    rows, width = shard.shape
    full = jnp.zeros((far, 2, 2, 2, rows, width), shard.dtype)
    for first, last, order in column_halves(width):
        part = shard[:, first:last]
        if far <= 4:
            held = jnp.zeros((far, rows, last - first), shard.dtype)
            held = lax.dynamic_update_slice(held, part[None], (mine_far, 0, 0))
            for step in range(1, far):
                moved = swapped(part, count, 8 * step)
                held = lax.dynamic_update_slice(held, moved[None], (mine_far ^ step, 0, 0))
        else:
            held = lax.all_gather(part, "dev", axis=0, axis_index_groups=far_groups(count))
        pieces = [(0, held)]
        for mask in order + (1,):
            pieces = pieces + [(seen | mask, swapped(piece, count, mask)) for seen, piece in pieces]
        for seen, piece in pieces:
            spot = {bit: bits[bit] ^ (1 if seen & bit else 0) for bit in (1, 2, 4)}
            full = lax.dynamic_update_slice(
                full, piece[:, None, None, None], (0, spot[4], spot[2], spot[1], 0, first)
            )
    return full.reshape(count * rows, width)


def scatter_start(grad):
    count = lax.axis_size("dev")
    mine = place_bits(lax.axis_index("dev"))[1]
    rows = grad.shape[0] // count
    split = grad.astype(jnp.bfloat16).reshape(count // 2, 2, rows, grad.shape[1])
    given = lax.dynamic_slice_in_dim(split, 1 - mine, 1, axis=1)
    taken = swapped(given, count, 1)
    kept = lax.dynamic_slice_in_dim(split, mine, 1, axis=1)
    return (kept.astype(jnp.float32) + taken.astype(jnp.float32)).astype(jnp.bfloat16)


def scatter_rest(half):
    count = lax.axis_size("dev")
    dev_index = lax.axis_index("dev")
    bits = place_bits(dev_index)
    far = count // 8
    mine_far = dev_index // 8
    rows, width = half.shape[2:]
    whole = half.reshape(far, 2, 2, rows, width)
    outs = []
    for first, last, order in column_halves(width):
        part = whole[..., first:last]
        for mask in order[::-1]:
            axis = 1 if mask == 4 or part.ndim == 4 else 2
            given = lax.dynamic_index_in_dim(part, 1 - bits[mask], axis, keepdims=False)
            kept = lax.dynamic_index_in_dim(part, bits[mask], axis, keepdims=False)
            taken = swapped(given, count, mask)
            part = (kept.astype(jnp.float32) + taken.astype(jnp.float32)).astype(jnp.bfloat16)
        if far <= 4:
            total = lax.dynamic_index_in_dim(part, mine_far, 0, keepdims=False).astype(jnp.float32)
            for step in range(1, far):
                given = lax.dynamic_index_in_dim(part, mine_far ^ step, 0, keepdims=False)
                total = total + swapped(given, count, 8 * step).astype(jnp.float32)
        else:
            total = lax.psum_scatter(
                part.reshape(far * rows, last - first),
                "dev",
                scatter_dimension=0,
                tiled=True,
                axis_index_groups=far_groups(count),
            ).astype(jnp.float32)
        outs.append(total)
    return jnp.concatenate(outs, axis=1)


def with_column(matrix, vector):
    return jnp.concatenate([matrix, jnp.pad(vector[:, None], ((0, 0), (0, 127)))], axis=1)


def layer_norm(values):
    centred = values - jnp.mean(values, axis=-1, keepdims=True)
    inverse_std = lax.rsqrt(jnp.mean(centred * centred, axis=-1, keepdims=True) + epsilon)
    return (centred * inverse_std, inverse_std)


def norm_back(grad_normed, normed, inverse_std):
    mean_grad = jnp.mean(grad_normed, axis=-1, keepdims=True)
    mean_mixed = jnp.mean(grad_normed * normed, axis=-1, keepdims=True)
    return inverse_std * (grad_normed - mean_grad - normed * mean_mixed)


def rope_tables(positions, head_size):
    half_size = head_size // 2
    inverse_freq = 10000.0 ** (-(jnp.arange(half_size).astype(jnp.float32) * 2.0 / head_size))
    angles = positions.astype(jnp.float32)[:, None] * inverse_freq[None, :]
    angles = jnp.concatenate([angles, angles], axis=-1)
    return (jnp.cos(angles)[:, None, :], jnp.sin(angles)[:, None, :])


def rotate_half(values):
    half_size = values.shape[-1] // 2
    return jnp.concatenate([-values[..., half_size:], values[..., :half_size]], axis=-1)


def unrotate_half(values):
    half_size = values.shape[-1] // 2
    return jnp.concatenate([values[..., half_size:], -values[..., :half_size]], axis=-1)


def apply_rope(values, cosine, sine_table):
    return values * cosine + rotate_half(values) * sine_table


def rope_back(grads_in, cosine, sine_table):
    return grads_in * cosine + unrotate_half(grads_in * sine_table)


def contract_rows(first_mat, second_mat):
    return lax.dot_general(
        first_mat, second_mat, (((0,), (0,)), ((), ())), preferred_element_type=jnp.float32
    )


def contract_cols(first_mat, second_mat):
    return lax.dot_general(
        first_mat, second_mat, (((1,), (1,)), ((), ())), preferred_element_type=jnp.float32
    )


def geglu(gate_part, up_part):
    return jax.nn.gelu(gate_part, approximate=False) * up_part


def local(tokens, seq_ids, positions, w_qkv, w_out, w_in, w_down, gain_attn, gain_mlp, cotangent):
    tok_rows, model_width = tokens.shape
    hidden_units = w_down.shape[0]
    head_count = model_width // HDIM
    dev_count = lax.axis_size("dev")
    dev_index = lax.axis_index("dev")
    query_block = math.gcd(tok_rows, 512)
    window_rows = query_block + 2 * HALF
    score_scale = 1.0 / math.sqrt(HDIM)
    block_total = tok_rows // query_block
    cosine, sine_table = rope_tables(positions, HDIM)
    key_ids = jnp.concatenate(
        [
            jnp.full((HALF,), seq_ids[0], jnp.int32),
            seq_ids,
            jnp.full((HALF,), seq_ids[-1], jnp.int32),
        ]
    )
    key_live = jnp.concatenate(
        [
            jnp.full((HALF,), dev_index > 0, jnp.bool_),
            jnp.ones((tok_rows,), jnp.bool_),
            jnp.full((HALF,), dev_index < dev_count - 1, jnp.bool_),
        ]
    )
    offsets = jnp.arange(query_block)[:, None] - jnp.arange(window_rows)[None, :] + HALF
    nearby = jnp.abs(offsets) <= HALF
    gains = jnp.pad(jnp.stack([gain_attn, gain_mlp], axis=1), ((0, 0), (0, 126)))
    qkv_and_gains = gather_rows(jnp.concatenate([w_qkv, gains], axis=1))
    full_qkv = qkv_and_gains[:, : 3 * model_width]
    full_gain_attn = qkv_and_gains[:, 3 * model_width]
    full_gain_mlp = qkv_and_gains[:, 3 * model_width + 1]
    out_and_in = gather_rows(jnp.concatenate([w_out, w_in], axis=1))
    full_out = out_and_in[:, :model_width]
    full_in = out_and_in[:, model_width:]
    down_rows = gather_rows(w_down.T)
    inputs = tokens.astype(jnp.float32)
    normed_attn, inv_attn = layer_norm(inputs)
    h_attn = (normed_attn * full_gain_attn.astype(jnp.float32)).astype(jnp.bfloat16)
    projected = jnp.dot(h_attn, full_qkv, preferred_element_type=jnp.float32).reshape(
        tok_rows, 3, head_count, HDIM
    )
    queries = apply_rope(projected[:, 0], cosine, sine_table).astype(jnp.bfloat16)
    keys_own = (
        apply_rope(projected[:, 1], cosine, sine_table)
        .astype(jnp.bfloat16)
        .reshape(tok_rows, model_width)
    )
    values_own = projected[:, 2].astype(jnp.bfloat16).reshape(tok_rows, model_width)
    key_values = padded(jnp.concatenate([keys_own, values_own], axis=1), (("dev", 0),), HALF)

    def block_scores(block_start):
        query_tile = queries[block_start : block_start + query_block]
        window = key_values[block_start : block_start + window_rows]
        key_tile = window[:, :model_width].reshape(window_rows, head_count, HDIM)
        value_tile = window[:, model_width:].reshape(window_rows, head_count, HDIM)
        query_ids = seq_ids[block_start : block_start + query_block]
        allowed = (
            nearby
            & (query_ids[:, None] == key_ids[None, block_start : block_start + window_rows])
            & key_live[None, block_start : block_start + window_rows]
        )
        scores = (
            jnp.einsum("qhd,khd->hqk", query_tile, key_tile, preferred_element_type=jnp.float32)
            * score_scale
        )
        scores = jnp.where(allowed[None], scores, masked_score)
        return (query_tile, key_tile, value_tile, scores)

    log_totals = []
    block_outputs = []
    for block_number in range(block_total):
        block_start = block_number * query_block
        query_tile, key_tile, value_tile, scores = block_scores(block_start)
        row_peak = jnp.max(scores, axis=-1, keepdims=True)
        exponent = jnp.exp(scores - row_peak)
        row_total = jnp.sum(exponent, axis=-1, keepdims=True)
        attn_probs = (exponent / row_total).astype(jnp.bfloat16)
        log_totals.append(row_peak + jnp.log(row_total))
        block_outputs.append(
            jnp.einsum(
                "hqk,khd->qhd", attn_probs, value_tile, preferred_element_type=jnp.float32
            ).reshape(query_block, model_width)
        )
    mixed = jnp.concatenate(block_outputs, axis=0).astype(jnp.bfloat16)
    residual = inputs + jnp.dot(mixed, full_out, preferred_element_type=jnp.float32)
    normed_mlp, inv_mlp = layer_norm(residual)
    h_mlp = (normed_mlp * full_gain_mlp.astype(jnp.float32)).astype(jnp.bfloat16)
    gate_up = jnp.dot(h_mlp, full_in, preferred_element_type=jnp.float32)
    gate_part = gate_up[:, :hidden_units]
    up_part = gate_up[:, hidden_units:]
    activated = geglu(gate_part, up_part).astype(jnp.bfloat16)
    layer_out = (
        residual + contract_cols(activated, down_rows)
    ).astype(jnp.bfloat16)
    down_half = scatter_start(contract_rows(cotangent, activated))
    d_activated = jnp.dot(cotangent, down_rows, preferred_element_type=jnp.float32)
    _, geglu_back = jax.vjp(geglu, gate_part, up_part)
    d_gate, d_up = geglu_back(d_activated)
    d_gate_up = jnp.concatenate([d_gate, d_up], axis=1).astype(jnp.bfloat16)
    d_gate_up, down_half = lax.optimization_barrier((d_gate_up, down_half))
    down_part = scatter_rest(down_half).T
    in_grad = contract_rows(h_mlp, d_gate_up)
    d_h_mlp = contract_cols(d_gate_up, full_in)
    mlp_gain_grad = jnp.sum(d_h_mlp * normed_mlp, axis=0)
    in_half = scatter_start(with_column(in_grad, mlp_gain_grad))
    d_residual = cotangent.astype(jnp.float32) + norm_back(
        d_h_mlp * full_gain_mlp.astype(jnp.float32), normed_mlp, inv_mlp
    )
    d_branch = d_residual.astype(jnp.bfloat16)
    out_half = scatter_start(contract_rows(mixed, d_branch))
    d_branch, in_half, out_half = lax.optimization_barrier((d_branch, in_half, out_half))
    in_sums = scatter_rest(in_half)
    in_part, mlp_gain_part = in_sums[:, : 2 * hidden_units], in_sums[:, 2 * hidden_units]
    out_part = scatter_rest(out_half)
    d_mixed = contract_cols(d_branch, full_out).astype(jnp.bfloat16)
    d_query_list = []
    d_window = jnp.zeros((tok_rows + 2 * HALF, 2 * model_width), jnp.float32)
    for block_number in range(block_total):
        block_start = block_number * query_block
        query_tile, key_tile, value_tile, scores = block_scores(block_start)
        attn_probs = jnp.exp(scores - log_totals[block_number])
        grad_tile = d_mixed[block_start : block_start + query_block].reshape(
            query_block, head_count, HDIM
        )
        d_probs = jnp.einsum(
            "qhd,khd->hqk", grad_tile, value_tile, preferred_element_type=jnp.float32
        )
        d_scores = (
            attn_probs * (d_probs - jnp.sum(attn_probs * d_probs, axis=-1, keepdims=True))
        ).astype(jnp.bfloat16)
        d_query_list.append(
            jnp.einsum("hqk,khd->qhd", d_scores, key_tile, preferred_element_type=jnp.float32)
            * score_scale
        )
        d_keys = (
            jnp.einsum("hqk,qhd->khd", d_scores, query_tile, preferred_element_type=jnp.float32)
            * score_scale
        )
        d_values = jnp.einsum(
            "hqk,qhd->khd",
            attn_probs.astype(jnp.bfloat16),
            grad_tile,
            preferred_element_type=jnp.float32,
        )
        window_grad = jnp.concatenate(
            [d_keys.reshape(window_rows, model_width), d_values.reshape(window_rows, model_width)],
            axis=1,
        )
        d_window = d_window.at[block_start : block_start + window_rows].add(window_grad)
    from_right = passed_along(d_window[:HALF].astype(jnp.bfloat16), "dev", -1).astype(jnp.float32)
    from_left = passed_along(d_window[tok_rows + HALF :].astype(jnp.bfloat16), "dev", 1).astype(
        jnp.float32
    )
    d_own = d_window[HALF : tok_rows + HALF]
    d_own = d_own.at[:HALF].add(from_left).at[tok_rows - HALF :].add(from_right)
    d_query_all = jnp.concatenate(d_query_list, axis=0)
    d_key_all = d_own[:, :model_width].reshape(tok_rows, head_count, HDIM)
    d_projected = jnp.concatenate(
        [
            rope_back(d_query_all, cosine, sine_table).reshape(tok_rows, model_width),
            rope_back(d_key_all, cosine, sine_table).reshape(tok_rows, model_width),
            d_own[:, model_width:],
        ],
        axis=1,
    ).astype(jnp.bfloat16)
    d_h_attn = contract_cols(d_projected, full_qkv)
    attn_gain_grad = jnp.sum(d_h_attn * normed_attn, axis=0)
    tokens_grad = (
        d_residual + norm_back(d_h_attn * full_gain_attn.astype(jnp.float32), normed_attn, inv_attn)
    ).astype(jnp.bfloat16)
    qkv_grad = contract_rows(h_attn, d_projected)
    qkv_sums = scatter_rest(scatter_start(with_column(qkv_grad, attn_gain_grad)))
    qkv_part, attn_gain_part = qkv_sums[:, : 3 * model_width], qkv_sums[:, 3 * model_width]
    return (
        layer_out,
        tokens_grad,
        qkv_part,
        out_part,
        in_part,
        down_part,
        attn_gain_part,
        mlp_gain_part,
    )


def solution(mesh):
    return jax.shard_map(
        local,
        mesh=mesh,
        in_specs=(
            P("dev", None),
            P("dev"),
            P("dev"),
            P("dev", None),
            P("dev", None),
            P("dev", None),
            P(None, "dev"),
            P("dev"),
            P("dev"),
            P("dev", None),
        ),
        out_specs=(
            P("dev", None),
            P("dev", None),
            P("dev", None),
            P("dev", None),
            P("dev", None),
            P(None, "dev"),
            P("dev"),
            P("dev"),
        ),
        check_vma=False,
    )
```

```python
import math

import jax
import jax.numpy as jnp
from jax import lax
from jax.sharding import PartitionSpec as P

HDIM = 64
HALF = 64


epsilon = 1e-05
masked_score = -1e30


def padded(cells, sides, width):
    for axis, dim in sides:
        count = lax.axis_size(axis)
        ends = count - 1
        head = lax.slice_in_dim(cells, 0, width, axis=dim)
        tail = lax.slice_in_dim(cells, cells.shape[dim] - width, cells.shape[dim], axis=dim)
        cells = jnp.concatenate(
            [
                lax.ppermute(tail, axis, [(i, (i + 1) % count) for i in range(ends)]),
                cells,
                lax.ppermute(head, axis, [((i + 1) % count, i) for i in range(ends)]),
            ],
            axis=dim,
        )
    return cells


def passed_along(value, axis, steps):
    count = lax.axis_size(axis)
    leading, last = (max(0, -steps), min(count, count - steps))
    return lax.ppermute(value, axis, [(source, source + steps) for source in range(leading, last)])


def swapped(value, count, mask):
    return lax.ppermute(value, "dev", [(i, i ^ mask) for i in range(count)])


def column_halves(width):
    middle = max(128, (width // 256) * 128)
    return ((0, middle, (2, 4)), (middle, width, (4, 2)))


def place_bits(dev_index):
    return {1: dev_index % 2, 2: (dev_index // 2) % 2, 4: (dev_index // 4) % 2}


def far_groups(count):
    return [list(range(first, count, 8)) for first in range(8)]


def gather_far(shard):
    count = lax.axis_size("dev")
    far = count // 8
    mine_far = lax.axis_index("dev") // 8
    halves = []
    for first, last, _ in column_halves(shard.shape[1]):
        part = shard[:, first:last]
        if far <= 4:
            held = jnp.zeros((far,) + part.shape, shard.dtype)
            held = lax.dynamic_update_slice(held, part[None], (mine_far, 0, 0))
            for step in range(1, far):
                moved = swapped(part, count, 8 * step)
                held = lax.dynamic_update_slice(held, moved[None], (mine_far ^ step, 0, 0))
        else:
            held = lax.all_gather(part, "dev", axis=0, axis_index_groups=far_groups(count))
        halves.append([held])
    return halves


def gather_near(halves, stage):
    count = lax.axis_size("dev")
    width = sum(pieces[0].shape[-1] for pieces in halves)
    return [
        pieces + [swapped(piece, count, order[stage]) for piece in pieces]
        for pieces, (_, _, order) in zip(halves, column_halves(width))
    ]


def gather_last(halves):
    count = lax.axis_size("dev")
    bits = place_bits(lax.axis_index("dev"))
    far, rows, _ = halves[0][0].shape
    width = sum(pieces[0].shape[-1] for pieces in halves)
    full = jnp.zeros((far, 2, 2, 2, rows, width), halves[0][0].dtype)
    for pieces, (first, _, order) in zip(halves, column_halves(width)):
        for place, piece in enumerate(pieces):
            seen = (order[0] if place & 1 else 0) + (order[1] if place & 2 else 0)
            for core, block in ((0, piece), (1, swapped(piece, count, 1))):
                spot = {bit: bits[bit] ^ (1 if (seen + core) & bit else 0) for bit in (1, 2, 4)}
                full = lax.dynamic_update_slice(
                    full, block[:, None, None, None], (0, spot[4], spot[2], spot[1], 0, first)
                )
    return full.reshape(count * rows, width)


def scatter_start(grad):
    count = lax.axis_size("dev")
    mine = place_bits(lax.axis_index("dev"))[1]
    rows = grad.shape[0] // count
    split = grad.astype(jnp.bfloat16).reshape(count // 2, 2, rows, grad.shape[1])
    given = lax.dynamic_slice_in_dim(split, 1 - mine, 1, axis=1)
    taken = swapped(given, count, 1)
    kept = lax.dynamic_slice_in_dim(split, mine, 1, axis=1)
    total = (kept.astype(jnp.float32) + taken.astype(jnp.float32)).astype(jnp.bfloat16)
    whole = total.reshape(count // 8, 2, 2, rows, grad.shape[1])
    return [whole[..., first:last] for first, last, _ in column_halves(grad.shape[1])]


def scatter_near(parts, stage):
    count = lax.axis_size("dev")
    bits = place_bits(lax.axis_index("dev"))
    width = sum(part.shape[-1] for part in parts)
    outs = []
    for part, (_, _, order) in zip(parts, column_halves(width)):
        mask = order[1 - stage]
        axis = 1 if mask == 4 or part.ndim == 4 else 2
        given = lax.dynamic_index_in_dim(part, 1 - bits[mask], axis, keepdims=False)
        kept = lax.dynamic_index_in_dim(part, bits[mask], axis, keepdims=False)
        taken = swapped(given, count, mask)
        outs.append((kept.astype(jnp.float32) + taken.astype(jnp.float32)).astype(jnp.bfloat16))
    return outs


def scatter_far(parts):
    count = lax.axis_size("dev")
    far = count // 8
    mine_far = lax.axis_index("dev") // 8
    outs = []
    for part in parts:
        if far <= 4:
            total = lax.dynamic_index_in_dim(part, mine_far, 0, keepdims=False).astype(jnp.float32)
            for step in range(1, far):
                given = lax.dynamic_index_in_dim(part, mine_far ^ step, 0, keepdims=False)
                total = total + swapped(given, count, 8 * step).astype(jnp.float32)
        else:
            total = lax.psum_scatter(
                part.reshape(-1, part.shape[-1]),
                "dev",
                scatter_dimension=0,
                tiled=True,
                axis_index_groups=far_groups(count),
            ).astype(jnp.float32)
        outs.append(total)
    return jnp.concatenate(outs, axis=1)


def tie(*values):
    return lax.optimization_barrier(values)


def layer_norm(values):
    centred = values - jnp.mean(values, axis=-1, keepdims=True)
    inverse_std = lax.rsqrt(jnp.mean(centred * centred, axis=-1, keepdims=True) + epsilon)
    return (centred * inverse_std, inverse_std)


def norm_back(grad_normed, normed, inverse_std):
    mean_grad = jnp.mean(grad_normed, axis=-1, keepdims=True)
    mean_mixed = jnp.mean(grad_normed * normed, axis=-1, keepdims=True)
    return inverse_std * (grad_normed - mean_grad - normed * mean_mixed)


def rope_tables(positions, head_size):
    half_size = head_size // 2
    inverse_freq = 10000.0 ** (-(jnp.arange(half_size).astype(jnp.float32) * 2.0 / head_size))
    angles = positions.astype(jnp.float32)[:, None] * inverse_freq[None, :]
    angles = jnp.concatenate([angles, angles], axis=-1)
    return (jnp.cos(angles)[:, None, :], jnp.sin(angles)[:, None, :])


def rotate_half(values):
    half_size = values.shape[-1] // 2
    return jnp.concatenate([-values[..., half_size:], values[..., :half_size]], axis=-1)


def unrotate_half(values):
    half_size = values.shape[-1] // 2
    return jnp.concatenate([values[..., half_size:], -values[..., :half_size]], axis=-1)


def apply_rope(values, cosine, sine_table):
    return values * cosine + rotate_half(values) * sine_table


def rope_back(grads_in, cosine, sine_table):
    return grads_in * cosine + unrotate_half(grads_in * sine_table)


def contract_rows(first_mat, second_mat):
    return lax.dot_general(
        first_mat, second_mat, (((0,), (0,)), ((), ())), preferred_element_type=jnp.float32
    )


def contract_cols(first_mat, second_mat):
    return lax.dot_general(
        first_mat, second_mat, (((1,), (1,)), ((), ())), preferred_element_type=jnp.float32
    )


def geglu(gate_part, up_part):
    return jax.nn.gelu(gate_part, approximate=False) * up_part


def local(tokens, seq_ids, positions, w_qkv, w_out, w_in, w_down, gain_attn, gain_mlp, cotangent):
    tok_rows, model_width = tokens.shape
    hidden_units = w_down.shape[0]
    head_count = model_width // HDIM
    dev_count = lax.axis_size("dev")
    dev_index = lax.axis_index("dev")
    query_block = math.gcd(tok_rows, 512)
    window_rows = query_block + 2 * HALF
    score_scale = 1.0 / math.sqrt(HDIM)
    block_total = tok_rows // query_block
    cosine, sine_table = rope_tables(positions, HDIM)
    key_ids = jnp.concatenate(
        [
            jnp.full((HALF,), seq_ids[0], jnp.int32),
            seq_ids,
            jnp.full((HALF,), seq_ids[-1], jnp.int32),
        ]
    )
    key_live = jnp.concatenate(
        [
            jnp.full((HALF,), dev_index > 0, jnp.bool_),
            jnp.ones((tok_rows,), jnp.bool_),
            jnp.full((HALF,), dev_index < dev_count - 1, jnp.bool_),
        ]
    )
    offsets = jnp.arange(query_block)[:, None] - jnp.arange(window_rows)[None, :] + HALF
    nearby = jnp.abs(offsets) <= HALF
    gains = jnp.pad(jnp.stack([gain_attn, gain_mlp], axis=1), ((0, 0), (0, 126)))
    first_set = gather_near(gather_far(jnp.concatenate([w_qkv, gains], axis=1)), 0)
    first_set, second_shard = tie(first_set, jnp.concatenate([w_out, w_in], axis=1))
    second_set = gather_far(second_shard)
    qkv_and_gains = gather_last(gather_near(first_set, 1))
    full_qkv = qkv_and_gains[:, : 3 * model_width]
    full_gain_attn = qkv_and_gains[:, 3 * model_width]
    full_gain_mlp = qkv_and_gains[:, 3 * model_width + 1]
    inputs = tokens.astype(jnp.float32)
    normed_attn, inv_attn = layer_norm(inputs)
    h_attn = (normed_attn * full_gain_attn.astype(jnp.float32)).astype(jnp.bfloat16)
    projected = jnp.dot(h_attn, full_qkv, preferred_element_type=jnp.float32)
    projected, second_set = tie(projected, second_set)
    projected = projected.reshape(tok_rows, 3, head_count, HDIM)
    second_set = gather_near(second_set, 0)
    queries = apply_rope(projected[:, 0], cosine, sine_table).astype(jnp.bfloat16)
    keys_own = (
        apply_rope(projected[:, 1], cosine, sine_table)
        .astype(jnp.bfloat16)
        .reshape(tok_rows, model_width)
    )
    values_own = projected[:, 2].astype(jnp.bfloat16).reshape(tok_rows, model_width)
    key_values = padded(jnp.concatenate([keys_own, values_own], axis=1), (("dev", 0),), HALF)

    def block_scores(block_start, queries, key_values):
        query_tile = queries[block_start : block_start + query_block]
        window = key_values[block_start : block_start + window_rows]
        key_tile = window[:, :model_width].reshape(window_rows, head_count, HDIM)
        value_tile = window[:, model_width:].reshape(window_rows, head_count, HDIM)
        query_ids = seq_ids[block_start : block_start + query_block]
        allowed = (
            nearby
            & (query_ids[:, None] == key_ids[None, block_start : block_start + window_rows])
            & key_live[None, block_start : block_start + window_rows]
        )
        scores = (
            jnp.einsum("qhd,khd->hqk", query_tile, key_tile, preferred_element_type=jnp.float32)
            * score_scale
        )
        scores = jnp.where(allowed[None], scores, masked_score)
        return (query_tile, key_tile, value_tile, scores)

    log_totals = []
    block_outputs = []
    for block_number in range(block_total):
        block_start = block_number * query_block
        query_tile, key_tile, value_tile, scores = block_scores(block_start, queries, key_values)
        row_peak = jnp.max(scores, axis=-1, keepdims=True)
        exponent = jnp.exp(scores - row_peak)
        row_total = jnp.sum(exponent, axis=-1, keepdims=True)
        attn_probs = (exponent / row_total).astype(jnp.bfloat16)
        log_totals.append(row_peak + jnp.log(row_total))
        block_outputs.append(
            jnp.einsum(
                "hqk,khd->qhd", attn_probs, value_tile, preferred_element_type=jnp.float32
            )
            .reshape(query_block, model_width)
            .astype(jnp.bfloat16)
        )
        if block_number == 0:
            block_outputs[0], second_set, third_shard, queries = tie(
                block_outputs[0], second_set, w_down.T, queries
            )
            second_set = gather_near(second_set, 1)
            third_set = gather_far(third_shard)
    mixed = jnp.concatenate(block_outputs, axis=0)
    out_and_in = gather_last(second_set)
    full_out = out_and_in[:, :model_width]
    full_in = out_and_in[:, model_width:]
    third_set = gather_near(third_set, 0)
    branch = jnp.dot(mixed, full_out, preferred_element_type=jnp.float32)
    branch, third_set = tie(branch, third_set)
    residual = inputs + branch
    down_rows = gather_last(gather_near(third_set, 1))
    normed_mlp, inv_mlp = layer_norm(residual)
    h_mlp = (normed_mlp * full_gain_mlp.astype(jnp.float32)).astype(jnp.bfloat16)
    gate_up = jnp.dot(h_mlp, full_in, preferred_element_type=jnp.float32)
    gate_part = gate_up[:, :hidden_units]
    up_part = gate_up[:, hidden_units:]
    activated = geglu(gate_part, up_part).astype(jnp.bfloat16)
    layer_out = (
        residual + contract_cols(activated, down_rows)
    ).astype(jnp.bfloat16)
    down_parts = scatter_start(contract_rows(cotangent, activated))
    d_activated = jnp.dot(cotangent, down_rows, preferred_element_type=jnp.float32)
    _, geglu_back = jax.vjp(geglu, gate_part, up_part)
    d_gate, d_up = geglu_back(d_activated)
    d_gate_up = jnp.concatenate([d_gate, d_up], axis=1).astype(jnp.bfloat16)
    d_gate_up, down_parts = tie(d_gate_up, down_parts)
    down_parts = scatter_near(down_parts, 0)
    in_parts = scatter_start(contract_rows(h_mlp, d_gate_up))
    d_gate_up, in_parts, down_parts = tie(d_gate_up, in_parts, down_parts)
    in_parts = scatter_near(in_parts, 0)
    down_parts = scatter_near(down_parts, 1)
    d_h_mlp = contract_cols(d_gate_up, full_in)
    d_residual = cotangent.astype(jnp.float32) + norm_back(
        d_h_mlp * full_gain_mlp.astype(jnp.float32), normed_mlp, inv_mlp
    )
    d_branch = d_residual.astype(jnp.bfloat16)
    d_branch, in_parts, down_parts = tie(d_branch, in_parts, down_parts)
    in_parts = scatter_near(in_parts, 1)
    down_part = scatter_far(down_parts).T
    out_parts = scatter_start(contract_rows(mixed, d_branch))
    d_mixed = contract_cols(d_branch, full_out).astype(jnp.bfloat16)
    d_query_list = []
    d_window = jnp.zeros((tok_rows + 2 * HALF, 2 * model_width), jnp.float32)
    for block_number in range(block_total):
        block_start = block_number * query_block
        query_tile, key_tile, value_tile, scores = block_scores(block_start, queries, key_values)
        attn_probs = jnp.exp(scores - log_totals[block_number])
        grad_tile = d_mixed[block_start : block_start + query_block].reshape(
            query_block, head_count, HDIM
        )
        d_probs = jnp.einsum(
            "qhd,khd->hqk", grad_tile, value_tile, preferred_element_type=jnp.float32
        )
        d_scores = (
            attn_probs * (d_probs - jnp.sum(attn_probs * d_probs, axis=-1, keepdims=True))
        ).astype(jnp.bfloat16)
        d_query_list.append(
            jnp.einsum("hqk,khd->qhd", d_scores, key_tile, preferred_element_type=jnp.float32)
            * score_scale
        )
        d_keys = (
            jnp.einsum("hqk,qhd->khd", d_scores, query_tile, preferred_element_type=jnp.float32)
            * score_scale
        )
        d_values = jnp.einsum(
            "hqk,qhd->khd",
            attn_probs.astype(jnp.bfloat16),
            grad_tile,
            preferred_element_type=jnp.float32,
        )
        window_grad = jnp.concatenate(
            [d_keys.reshape(window_rows, model_width), d_values.reshape(window_rows, model_width)],
            axis=1,
        )
        if block_number == 0:
            d_mixed, window_grad, in_parts, out_parts = tie(
                d_mixed, window_grad, in_parts, out_parts
            )
            in_sums = scatter_far(in_parts)
            out_parts = scatter_near(out_parts, 0)
        d_window = d_window.at[block_start : block_start + window_rows].add(window_grad)
        if block_number == block_total - 1:
            d_window, in_part, out_parts = tie(d_window, in_sums, out_parts)
            out_parts = scatter_near(out_parts, 1)
    from_right = passed_along(d_window[:HALF].astype(jnp.bfloat16), "dev", -1).astype(jnp.float32)
    from_left = passed_along(d_window[tok_rows + HALF :].astype(jnp.bfloat16), "dev", 1).astype(
        jnp.float32
    )
    d_own = d_window[HALF : tok_rows + HALF]
    d_own = d_own.at[:HALF].add(from_left).at[tok_rows - HALF :].add(from_right)
    d_query_all = jnp.concatenate(d_query_list, axis=0)
    d_key_all = d_own[:, :model_width].reshape(tok_rows, head_count, HDIM)
    d_projected = jnp.concatenate(
        [
            rope_back(d_query_all, cosine, sine_table).reshape(tok_rows, model_width),
            rope_back(d_key_all, cosine, sine_table).reshape(tok_rows, model_width),
            d_own[:, model_width:],
        ],
        axis=1,
    ).astype(jnp.bfloat16)
    qkv_parts = scatter_start(contract_rows(h_attn, d_projected))
    out_part = scatter_far(out_parts)
    d_projected, qkv_parts = tie(d_projected, qkv_parts)
    qkv_part = scatter_far(scatter_near(scatter_near(qkv_parts, 0), 1))
    d_h_attn = contract_cols(d_projected, full_qkv)
    tokens_grad = (
        d_residual + norm_back(d_h_attn * full_gain_attn.astype(jnp.float32), normed_attn, inv_attn)
    ).astype(jnp.bfloat16)
    attn_gain_part = jnp.sum(w_qkv.astype(jnp.float32) * qkv_part, axis=1) / gain_attn.astype(
        jnp.float32
    )
    mlp_gain_part = jnp.sum(w_in.astype(jnp.float32) * in_part, axis=1) / gain_mlp.astype(
        jnp.float32
    )
    return (
        layer_out,
        tokens_grad,
        qkv_part,
        out_part,
        in_part,
        down_part,
        attn_gain_part,
        mlp_gain_part,
    )


def solution(mesh):
    return jax.shard_map(
        local,
        mesh=mesh,
        in_specs=(
            P("dev", None),
            P("dev"),
            P("dev"),
            P("dev", None),
            P("dev", None),
            P("dev", None),
            P(None, "dev"),
            P("dev"),
            P("dev"),
            P("dev", None),
        ),
        out_specs=(
            P("dev", None),
            P("dev", None),
            P("dev", None),
            P("dev", None),
            P("dev", None),
            P(None, "dev"),
            P("dev"),
            P("dev"),
        ),
        check_vma=False,
    )
```

```python
import math

import jax
import jax.numpy as jnp
from jax import lax
from jax.sharding import PartitionSpec as P

HDIM = 64
HALF = 64


epsilon = 1e-05
masked_score = -1e30


def padded(cells, sides, width):
    for axis, dim in sides:
        count = lax.axis_size(axis)
        ends = count - 1
        head = lax.slice_in_dim(cells, 0, width, axis=dim)
        tail = lax.slice_in_dim(cells, cells.shape[dim] - width, cells.shape[dim], axis=dim)
        cells = jnp.concatenate(
            [
                lax.ppermute(tail, axis, [(i, (i + 1) % count) for i in range(ends)]),
                cells,
                lax.ppermute(head, axis, [((i + 1) % count, i) for i in range(ends)]),
            ],
            axis=dim,
        )
    return cells


def passed_along(value, axis, steps):
    count = lax.axis_size(axis)
    leading, last = (max(0, -steps), min(count, count - steps))
    return lax.ppermute(value, axis, [(source, source + steps) for source in range(leading, last)])


def swapped(value, count, mask):
    return lax.ppermute(value, "dev", [(i, i ^ mask) for i in range(count)])


def column_halves(width):
    middle = max(128, (width // 256) * 128)
    return ((0, middle, (2, 4)), (middle, width, (4, 2)))


def place_bits(dev_index):
    return {1: dev_index % 2, 2: (dev_index // 2) % 2, 4: (dev_index // 4) % 2}


def far_groups(count):
    return [list(range(first, count, 8)) for first in range(8)]


def gather_far(shard):
    count = lax.axis_size("dev")
    far = count // 8
    mine_far = lax.axis_index("dev") // 8
    halves = []
    for first, last, _ in column_halves(shard.shape[1]):
        part = shard[:, first:last]
        if far <= 4:
            held = jnp.zeros((far,) + part.shape, shard.dtype)
            held = lax.dynamic_update_slice(held, part[None], (mine_far, 0, 0))
            for step in range(1, far):
                moved = swapped(part, count, 8 * step)
                held = lax.dynamic_update_slice(held, moved[None], (mine_far ^ step, 0, 0))
        else:
            held = lax.all_gather(part, "dev", axis=0, axis_index_groups=far_groups(count))
        halves.append([held])
    return halves


def gather_near(halves, stage):
    count = lax.axis_size("dev")
    width = sum(pieces[0].shape[-1] for pieces in halves)
    return [
        pieces + [swapped(piece, count, order[stage]) for piece in pieces]
        for pieces, (_, _, order) in zip(halves, column_halves(width))
    ]


def gather_last(halves):
    count = lax.axis_size("dev")
    bits = place_bits(lax.axis_index("dev"))
    far, rows, _ = halves[0][0].shape
    width = sum(pieces[0].shape[-1] for pieces in halves)
    full = jnp.zeros((far, 2, 2, 2, rows, width), halves[0][0].dtype)
    for pieces, (first, _, order) in zip(halves, column_halves(width)):
        for place, piece in enumerate(pieces):
            seen = (order[0] if place & 1 else 0) + (order[1] if place & 2 else 0)
            for core, block in ((0, piece), (1, swapped(piece, count, 1))):
                spot = {bit: bits[bit] ^ (1 if (seen + core) & bit else 0) for bit in (1, 2, 4)}
                full = lax.dynamic_update_slice(
                    full, block[:, None, None, None], (0, spot[4], spot[2], spot[1], 0, first)
                )
    return full.reshape(count * rows, width)


def scatter_start(grad):
    count = lax.axis_size("dev")
    mine = place_bits(lax.axis_index("dev"))[1]
    rows = grad.shape[0] // count
    split = grad.astype(jnp.bfloat16).reshape(count // 2, 2, rows, grad.shape[1])
    given = lax.dynamic_slice_in_dim(split, 1 - mine, 1, axis=1)
    taken = swapped(given, count, 1)
    kept = lax.dynamic_slice_in_dim(split, mine, 1, axis=1)
    total = (kept.astype(jnp.float32) + taken.astype(jnp.float32)).astype(jnp.bfloat16)
    whole = total.reshape(count // 8, 2, 2, rows, grad.shape[1])
    return [whole[..., first:last] for first, last, _ in column_halves(grad.shape[1])]


def scatter_near(parts, stage):
    count = lax.axis_size("dev")
    bits = place_bits(lax.axis_index("dev"))
    width = sum(part.shape[-1] for part in parts)
    outs = []
    for part, (_, _, order) in zip(parts, column_halves(width)):
        mask = order[1 - stage]
        axis = 1 if mask == 4 or part.ndim == 4 else 2
        given = lax.dynamic_index_in_dim(part, 1 - bits[mask], axis, keepdims=False)
        kept = lax.dynamic_index_in_dim(part, bits[mask], axis, keepdims=False)
        taken = swapped(given, count, mask)
        outs.append((kept.astype(jnp.float32) + taken.astype(jnp.float32)).astype(jnp.bfloat16))
    return outs


def scatter_far(parts):
    count = lax.axis_size("dev")
    far = count // 8
    mine_far = lax.axis_index("dev") // 8
    outs = []
    for part in parts:
        if far <= 4:
            total = lax.dynamic_index_in_dim(part, mine_far, 0, keepdims=False).astype(jnp.float32)
            for step in range(1, far):
                given = lax.dynamic_index_in_dim(part, mine_far ^ step, 0, keepdims=False)
                total = total + swapped(given, count, 8 * step).astype(jnp.float32)
        else:
            total = lax.psum_scatter(
                part.reshape(-1, part.shape[-1]),
                "dev",
                scatter_dimension=0,
                tiled=True,
                axis_index_groups=far_groups(count),
            ).astype(jnp.float32)
        outs.append(total)
    return jnp.concatenate(outs, axis=1)


def tie(*values):
    return lax.optimization_barrier(values)


def layer_norm(values):
    centred = values - jnp.mean(values, axis=-1, keepdims=True)
    inverse_std = lax.rsqrt(jnp.mean(centred * centred, axis=-1, keepdims=True) + epsilon)
    return (centred * inverse_std, inverse_std)


def norm_back(grad_normed, normed, inverse_std):
    mean_grad = jnp.mean(grad_normed, axis=-1, keepdims=True)
    mean_mixed = jnp.mean(grad_normed * normed, axis=-1, keepdims=True)
    return inverse_std * (grad_normed - mean_grad - normed * mean_mixed)


def rope_tables(positions, head_size):
    half_size = head_size // 2
    inverse_freq = 10000.0 ** (-(jnp.arange(half_size).astype(jnp.float32) * 2.0 / head_size))
    angles = positions.astype(jnp.float32)[:, None] * inverse_freq[None, :]
    angles = jnp.concatenate([angles, angles], axis=-1)
    return (jnp.cos(angles)[:, None, :], jnp.sin(angles)[:, None, :])


def rotate_half(values):
    half_size = values.shape[-1] // 2
    return jnp.concatenate([-values[..., half_size:], values[..., :half_size]], axis=-1)


def unrotate_half(values):
    half_size = values.shape[-1] // 2
    return jnp.concatenate([values[..., half_size:], -values[..., :half_size]], axis=-1)


def apply_rope(values, cosine, sine_table):
    return values * cosine + rotate_half(values) * sine_table


def rope_back(grads_in, cosine, sine_table):
    return grads_in * cosine + unrotate_half(grads_in * sine_table)


def contract_rows(first_mat, second_mat):
    return lax.dot_general(
        first_mat, second_mat, (((0,), (0,)), ((), ())), preferred_element_type=jnp.float32
    )


def contract_cols(first_mat, second_mat):
    return lax.dot_general(
        first_mat, second_mat, (((1,), (1,)), ((), ())), preferred_element_type=jnp.float32
    )


def geglu(gate_part, up_part):
    return jax.nn.gelu(gate_part, approximate=False) * up_part


def local(tokens, seq_ids, positions, w_qkv, w_out, w_in, w_down, gain_attn, gain_mlp, cotangent):
    tok_rows, model_width = tokens.shape
    hidden_units = w_down.shape[0]
    head_count = model_width // HDIM
    dev_count = lax.axis_size("dev")
    dev_index = lax.axis_index("dev")
    query_block = math.gcd(tok_rows, 512)
    window_rows = query_block + 2 * HALF
    score_scale = 1.0 / math.sqrt(HDIM)
    block_total = tok_rows // query_block
    cosine, sine_table = rope_tables(positions, HDIM)
    key_ids = jnp.concatenate(
        [
            jnp.full((HALF,), seq_ids[0], jnp.int32),
            seq_ids,
            jnp.full((HALF,), seq_ids[-1], jnp.int32),
        ]
    )
    key_live = jnp.concatenate(
        [
            jnp.full((HALF,), dev_index > 0, jnp.bool_),
            jnp.ones((tok_rows,), jnp.bool_),
            jnp.full((HALF,), dev_index < dev_count - 1, jnp.bool_),
        ]
    )
    offsets = jnp.arange(query_block)[:, None] - jnp.arange(window_rows)[None, :] + HALF
    nearby = jnp.abs(offsets) <= HALF
    gains = jnp.pad(jnp.stack([gain_attn, gain_mlp], axis=1), ((0, 0), (0, 126)))
    first_set = gather_near(gather_far(jnp.concatenate([w_qkv, gains], axis=1)), 0)
    first_set, second_shard = tie(first_set, jnp.concatenate([w_out, w_in], axis=1))
    second_set = gather_far(second_shard)
    qkv_and_gains = gather_last(gather_near(first_set, 1))
    full_qkv = qkv_and_gains[:, : 3 * model_width]
    full_gain_attn = qkv_and_gains[:, 3 * model_width]
    full_gain_mlp = qkv_and_gains[:, 3 * model_width + 1]
    inputs = tokens.astype(jnp.float32)
    normed_attn, inv_attn = layer_norm(inputs)
    h_attn = (normed_attn * full_gain_attn.astype(jnp.float32)).astype(jnp.bfloat16)
    projected = jnp.dot(h_attn, full_qkv, preferred_element_type=jnp.float32)
    _, second_set = tie(projected[:8, :128], second_set)
    projected = projected.reshape(tok_rows, 3, head_count, HDIM)
    second_set = gather_near(second_set, 0)
    queries = apply_rope(projected[:, 0], cosine, sine_table).astype(jnp.bfloat16)
    keys_own = (
        apply_rope(projected[:, 1], cosine, sine_table)
        .astype(jnp.bfloat16)
        .reshape(tok_rows, model_width)
    )
    values_own = projected[:, 2].astype(jnp.bfloat16).reshape(tok_rows, model_width)
    key_values = padded(jnp.concatenate([keys_own, values_own], axis=1), (("dev", 0),), HALF)

    def block_scores(block_start, queries, key_values):
        query_tile = queries[block_start : block_start + query_block]
        window = key_values[block_start : block_start + window_rows]
        key_tile = window[:, :model_width].reshape(window_rows, head_count, HDIM)
        value_tile = window[:, model_width:].reshape(window_rows, head_count, HDIM)
        query_ids = seq_ids[block_start : block_start + query_block]
        allowed = (
            nearby
            & (query_ids[:, None] == key_ids[None, block_start : block_start + window_rows])
            & key_live[None, block_start : block_start + window_rows]
        )
        scores = (
            jnp.einsum("qhd,khd->hqk", query_tile, key_tile, preferred_element_type=jnp.float32)
            * score_scale
        )
        scores = jnp.where(allowed[None], scores, masked_score)
        return (query_tile, key_tile, value_tile, scores)

    log_totals = []
    block_outputs = []
    for block_number in range(block_total):
        block_start = block_number * query_block
        query_tile, key_tile, value_tile, scores = block_scores(block_start, queries, key_values)
        row_peak = jnp.max(scores, axis=-1, keepdims=True)
        exponent = jnp.exp(scores - row_peak)
        row_total = jnp.sum(exponent, axis=-1, keepdims=True)
        attn_probs = (exponent / row_total).astype(jnp.bfloat16)
        log_totals.append(row_peak + jnp.log(row_total))
        block_outputs.append(
            jnp.einsum(
                "hqk,khd->qhd", attn_probs, value_tile, preferred_element_type=jnp.float32
            )
            .reshape(query_block, model_width)
            .astype(jnp.bfloat16)
        )
        if block_number == 0:
            block_outputs[0], second_set, third_shard, queries = tie(
                block_outputs[0], second_set, w_down.T, queries
            )
            second_set = gather_near(second_set, 1)
            third_set = gather_far(third_shard)
    mixed = jnp.concatenate(block_outputs, axis=0)
    out_and_in = gather_last(second_set)
    full_out = out_and_in[:, :model_width]
    full_in = out_and_in[:, model_width:]
    third_set = gather_near(third_set, 0)
    branch = jnp.dot(mixed, full_out, preferred_element_type=jnp.float32)
    branch, third_set = tie(branch, third_set)
    residual = inputs + branch
    down_rows = gather_last(gather_near(third_set, 1))
    normed_mlp, inv_mlp = layer_norm(residual)
    h_mlp = (normed_mlp * full_gain_mlp.astype(jnp.float32)).astype(jnp.bfloat16)
    gate_up = jnp.dot(h_mlp, full_in, preferred_element_type=jnp.float32)
    gate_part = gate_up[:, :hidden_units]
    up_part = gate_up[:, hidden_units:]
    activated = geglu(gate_part, up_part).astype(jnp.bfloat16)
    layer_out = (
        residual + contract_cols(activated, down_rows)
    ).astype(jnp.bfloat16)
    down_parts = scatter_start(contract_rows(cotangent, activated))
    d_activated = jnp.dot(cotangent, down_rows, preferred_element_type=jnp.float32)
    _, geglu_back = jax.vjp(geglu, gate_part, up_part)
    d_gate, d_up = geglu_back(d_activated)
    d_gate_up = jnp.concatenate([d_gate, d_up], axis=1).astype(jnp.bfloat16)
    d_gate_up, down_parts = tie(d_gate_up, down_parts)
    down_parts = scatter_near(down_parts, 0)
    in_parts = scatter_start(contract_rows(h_mlp, d_gate_up))
    d_gate_up, in_parts, down_parts = tie(d_gate_up, in_parts, down_parts)
    in_parts = scatter_near(in_parts, 0)
    down_parts = scatter_near(down_parts, 1)
    d_h_mlp = contract_cols(d_gate_up, full_in)
    d_residual = cotangent.astype(jnp.float32) + norm_back(
        d_h_mlp * full_gain_mlp.astype(jnp.float32), normed_mlp, inv_mlp
    )
    d_branch = d_residual.astype(jnp.bfloat16)
    d_branch, in_parts, down_parts = tie(d_branch, in_parts, down_parts)
    in_parts = scatter_near(in_parts, 1)
    down_part = scatter_far(down_parts).T
    out_parts = scatter_start(contract_rows(mixed, d_branch))
    d_mixed = contract_cols(d_branch, full_out).astype(jnp.bfloat16)
    d_query_list = []
    d_window = jnp.zeros((tok_rows + 2 * HALF, 2 * model_width), jnp.float32)
    for block_number in range(block_total):
        block_start = block_number * query_block
        query_tile, key_tile, value_tile, scores = block_scores(block_start, queries, key_values)
        attn_probs = jnp.exp(scores - log_totals[block_number])
        grad_tile = d_mixed[block_start : block_start + query_block].reshape(
            query_block, head_count, HDIM
        )
        d_probs = jnp.einsum(
            "qhd,khd->hqk", grad_tile, value_tile, preferred_element_type=jnp.float32
        )
        d_scores = (
            attn_probs * (d_probs - jnp.sum(attn_probs * d_probs, axis=-1, keepdims=True))
        ).astype(jnp.bfloat16)
        d_query_list.append(
            jnp.einsum("hqk,khd->qhd", d_scores, key_tile, preferred_element_type=jnp.float32)
            * score_scale
        )
        d_keys = (
            jnp.einsum("hqk,qhd->khd", d_scores, query_tile, preferred_element_type=jnp.float32)
            * score_scale
        )
        d_values = jnp.einsum(
            "hqk,qhd->khd",
            attn_probs.astype(jnp.bfloat16),
            grad_tile,
            preferred_element_type=jnp.float32,
        )
        window_grad = jnp.concatenate(
            [d_keys.reshape(window_rows, model_width), d_values.reshape(window_rows, model_width)],
            axis=1,
        )
        if block_number == 0:
            d_mixed, window_grad, in_parts, out_parts = tie(
                d_mixed, window_grad, in_parts, out_parts
            )
            in_sums = scatter_far(in_parts)
            out_parts = scatter_near(out_parts, 0)
        d_window = d_window.at[block_start : block_start + window_rows].add(window_grad)
        if block_number == block_total - 1:
            d_window, in_part, out_parts = tie(d_window, in_sums, out_parts)
            out_parts = scatter_near(out_parts, 1)
    from_right = passed_along(d_window[:HALF].astype(jnp.bfloat16), "dev", -1).astype(jnp.float32)
    from_left = passed_along(d_window[tok_rows + HALF :].astype(jnp.bfloat16), "dev", 1).astype(
        jnp.float32
    )
    d_own = d_window[HALF : tok_rows + HALF]
    d_own = d_own.at[:HALF].add(from_left).at[tok_rows - HALF :].add(from_right)
    d_query_all = jnp.concatenate(d_query_list, axis=0)
    d_key_all = d_own[:, :model_width].reshape(tok_rows, head_count, HDIM)
    d_projected = jnp.concatenate(
        [
            rope_back(d_query_all, cosine, sine_table).reshape(tok_rows, model_width),
            rope_back(d_key_all, cosine, sine_table).reshape(tok_rows, model_width),
            d_own[:, model_width:],
        ],
        axis=1,
    ).astype(jnp.bfloat16)
    qkv_parts = scatter_start(contract_rows(h_attn, d_projected))
    out_part = scatter_far(out_parts)
    d_projected, qkv_parts = tie(d_projected, qkv_parts)
    qkv_part = scatter_far(scatter_near(scatter_near(qkv_parts, 0), 1))
    d_h_attn = contract_cols(d_projected, full_qkv)
    tokens_grad = (
        d_residual + norm_back(d_h_attn * full_gain_attn.astype(jnp.float32), normed_attn, inv_attn)
    ).astype(jnp.bfloat16)
    attn_gain_part = jnp.sum(w_qkv.astype(jnp.float32) * qkv_part, axis=1) / gain_attn.astype(
        jnp.float32
    )
    mlp_gain_part = jnp.sum(w_in.astype(jnp.float32) * in_part, axis=1) / gain_mlp.astype(
        jnp.float32
    )
    return (
        layer_out,
        tokens_grad,
        qkv_part,
        out_part,
        in_part,
        down_part,
        attn_gain_part,
        mlp_gain_part,
    )


def solution(mesh):
    return jax.shard_map(
        local,
        mesh=mesh,
        in_specs=(
            P("dev", None),
            P("dev"),
            P("dev"),
            P("dev", None),
            P("dev", None),
            P("dev", None),
            P(None, "dev"),
            P("dev"),
            P("dev"),
            P("dev", None),
        ),
        out_specs=(
            P("dev", None),
            P("dev", None),
            P("dev", None),
            P("dev", None),
            P("dev", None),
            P(None, "dev"),
            P("dev"),
            P("dev"),
        ),
        check_vma=False,
    )
```
